32 devices in a mesh: groups: 2 (over x), lon: 16 (over z, y, core).
Axes of the slice: x: 2, y: 2, z: 4, core: 2. Of those that a mesh axis runs over, the one named last changes fastest.
Arguments:
- queries: bfloat16 [96, 192, 512], P('groups', 'lon'), parts along dimension 0, may hold values from -8 to 8
- key_vectors: bfloat16 [96, 192, 512], P('groups', 'lon'), parts along dimension 0, may hold values from -8 to 8
- value_vectors: bfloat16 [96, 192, 512], P('groups', 'lon'), parts along dimension 0, may hold values from -6 to 6
- out_weight: bfloat16 [512, 512], replicated, may hold values from -0.25 to 0.25
- lat_window: int32 [96], P('groups'), parts along dimension 0, may hold values from 0 to 5, as said below
- lon_offset: int32 [96], P('groups'), parts along dimension 0, may hold values from 0 to 11, as said below
- cotangent: bfloat16 [96, 192, 512], P('groups', 'lon'), parts along dimension 0, may hold values from -6 to 6
Outputs:
- block_out: bfloat16 [96, 192, 512], P('groups', 'lon'), parts along dimension 0
- grad_queries: bfloat16 [96, 192, 512], P('groups', 'lon'), parts along dimension 0
- grad_keys: bfloat16 [96, 192, 512], P('groups', 'lon'), parts along dimension 0
- grad_values: bfloat16 [96, 192, 512], P('groups', 'lon'), parts along dimension 0
- grad_out_weight: float32 [1024, 512], P('groups'), parts along dimension 0
The draws below stay inside these ranges and needn't reach their ends.
There are 2 independent parts, one for each index of `groups`. The reference program is written for one: setup_inputs(seed, part) draws one part's arguments, and reference() takes and returns one part's arrays. A program takes and returns all parts, laid end to end along the dimension named above; an argument that names none is the same for every part. Nothing has to cross between parts.
Inputs may be any that keep to these rules, and one draw needn't show every extreme that they name: `lat_window`: each aligned block of 24 rows holds three latitude windows of consecutive rows, numbered in order, one of them 12 rows long. `lon_offset`: the same for all rows of one latitude window; 11 in some window of every draw.
All inputs are finite; a program needn't handle non-finite values.
Results may differ from the reference program's by a relative error of at most 0.017.
Values may be sent and summed in bfloat16 or wider, within the bound.
No kernel may reach another device: no remote copies, remote signals or barrier semaphores. Data moves between devices by JAX's collectives and lax.ppermute only.
A program may use at most 128 MiB of HBM per device.

```python
import jax
import jax.numpy as jnp
from jax import lax

C = 512
HD = 32
WIN = 12
LAT_ROWS = 48
WIDTH_LON = 192


def window_layout(key):
    blocks = LAT_ROWS // (2 * WIN)
    picker = jax.random.fold_in(key, 11)
    first_key, second_key, third_key = jax.random.split(picker, 3)
    middle = jax.random.randint(first_key, (blocks,), 1, WIN)
    turning = jax.random.randint(second_key, (blocks,), 0, 3)
    lengths_base = jnp.stack([jnp.full((blocks,), WIN, jnp.int32), middle, WIN - middle], axis=1)
    rotation = (jnp.arange(3, dtype=jnp.int32)[None, :] - turning[:, None]) % 3
    lengths = jnp.take_along_axis(lengths_base, rotation, axis=1)
    ends = jnp.cumsum(lengths, axis=1)
    local_rows = jnp.arange(2 * WIN, dtype=jnp.int32)
    inside = jnp.sum((local_rows[None, :, None] >= ends[:, None, :]).astype(jnp.int32), axis=2)
    ids = inside + 3 * jnp.arange(blocks, dtype=jnp.int32)[:, None]
    offsets = jax.random.randint(third_key, (blocks * 3,), 0, WIN)
    chosen = jax.random.randint(jax.random.fold_in(picker, 5), (), 0, blocks * 3)
    offsets = jnp.where(jnp.arange(blocks * 3) == chosen, WIN - 1, offsets)
    return (ids.reshape(-1).astype(jnp.int32), offsets.astype(jnp.int32))


def draw_lat_window(key, part):
    return window_layout(key)[0]


def draw_lon_offset(key, part):
    ids, offsets = window_layout(key)
    return jnp.take(offsets, ids).astype(jnp.int32)


def drawn_pair(key):
    shape = (LAT_ROWS, WIDTH_LON, C)
    query_out = jax.random.truncated_normal(jax.random.fold_in(key, 1), -8.0, 8.0, shape, jnp.float32)
    key_out = jax.random.truncated_normal(jax.random.fold_in(key, 2), -8.0, 8.0, shape, jnp.float32)
    return (query_out, key_out)


def draw_queries(key, part):
    return drawn_pair(key)[0].astype(jnp.bfloat16)


def draw_key_vectors(key, part):
    return drawn_pair(key)[1].astype(jnp.bfloat16)


def block_levels(stream_key, dims, shards, smallest, top_value):
    level = 1.0
    for dim, parts in shards:
        steps = jax.random.uniform(jax.random.fold_in(jax.random.fold_in(stream_key, 6), dim), (parts,), jnp.float32, smallest / len(shards), top_value / len(shards))
        level = level * jnp.repeat(jnp.exp(steps), dims[dim] // parts).reshape((-1,) + (1,) * (len(dims) - 1 - dim))
    return level


def centred(stream_key, dims, deviation, reach, cuts=(), kind=jnp.bfloat16):
    drawn = deviation * jax.random.normal(stream_key, dims, jnp.float32)
    if cuts:
        drawn = drawn * block_levels(stream_key, dims, cuts, -0.22, 0.18)
    return jnp.clip(drawn, -reach, reach).astype(kind)


def setup_inputs(seed: int = 0, part: int = 0) -> dict:
    keys = jax.random.split(jax.random.key(seed), 8)
    part_keys = jax.random.split(jax.random.fold_in(keys[7], part), 8)
    return {
        "queries": draw_queries(jax.random.fold_in(jax.random.fold_in(keys[7], part), 71), part),
        "key_vectors": draw_key_vectors(jax.random.fold_in(jax.random.fold_in(keys[7], part), 71), part),
        "value_vectors": centred(part_keys[2], (LAT_ROWS, WIDTH_LON, C), 1.0, 6.0, ((1, 16),)),
        "out_weight": centred(keys[3], (C, C), C ** -0.5, 0.25),
        "lat_window": draw_lat_window(jax.random.fold_in(jax.random.fold_in(keys[7], part), 71), part),
        "lon_offset": draw_lon_offset(jax.random.fold_in(jax.random.fold_in(keys[7], part), 71), part),
        "cotangent": centred(part_keys[6], (LAT_ROWS, WIDTH_LON, C), 1.0, 6.0, ((1, 16),)),
    }


def to_blocks(source, head_count):
    row_count, col_count, channels = source.shape
    shaped = source.reshape(row_count // (2 * WIN), 2 * WIN, col_count // WIN, WIN, head_count, channels // head_count)
    shaped = shaped.transpose(0, 2, 1, 3, 4, 5)
    return shaped.reshape(-1, 2 * WIN * WIN, head_count, channels // head_count)


def from_blocks(blocks, row_count, col_count):
    channels = blocks.shape[2] * blocks.shape[3]
    shaped = blocks.reshape(row_count // (2 * WIN), col_count // WIN, 2 * WIN, WIN, channels)
    shaped = shaped.transpose(0, 2, 1, 3, 4)
    return shaped.reshape(row_count, col_count, channels)


def block_ids(lat_window, col_count):
    row_count = lat_window.shape[0]
    shaped = lat_window.reshape(row_count // (2 * WIN), 1, 2 * WIN, 1)
    shaped = jnp.broadcast_to(shaped, (row_count // (2 * WIN), col_count // WIN, 2 * WIN, WIN))
    return shaped.reshape(-1, 2 * WIN * WIN)


def window_pass(pieces):
    query_blk, key_blk, value_blk, grad_blk, window_ids = pieces
    query_f = query_blk.astype(jnp.float32)
    key_f = key_blk.astype(jnp.float32)
    value_f = value_blk.astype(jnp.float32)
    grad_f = grad_blk.astype(jnp.float32)
    scaling = float(HD) ** -0.5
    scores = jnp.einsum('qhd,khd->hqk', query_f, key_f) * scaling
    allowed = window_ids[:, None] == window_ids[None, :]
    scores = jnp.where(allowed[None], scores, -1e30)
    row_max = jnp.max(scores, axis=2, keepdims=True)
    exponent = jnp.exp(scores - row_max)
    weights_full = exponent / jnp.sum(exponent, axis=2, keepdims=True)
    weights_round = weights_full.astype(jnp.bfloat16).astype(jnp.float32)
    attended = jnp.einsum('hqk,khd->qhd', weights_round, value_f).astype(jnp.bfloat16)
    grad_probs = jnp.einsum('qhd,khd->hqk', grad_f, value_f)
    grad_value = jnp.einsum('hqk,qhd->khd', weights_round, grad_f).astype(jnp.bfloat16)
    inner = jnp.sum(weights_full * grad_probs, axis=2, keepdims=True)
    grad_scores = (weights_full * (grad_probs - inner) * scaling).astype(jnp.bfloat16).astype(jnp.float32)
    grad_query = jnp.einsum('hqk,khd->qhd', grad_scores, key_f).astype(jnp.bfloat16)
    grad_key = jnp.einsum('hqk,qhd->khd', grad_scores, query_f).astype(jnp.bfloat16)
    return attended, grad_query, grad_key, grad_value


def pick_cols(source, index):
    return jnp.take_along_axis(source, index[:, :, None], axis=1)


def reference(queries, key_vectors, value_vectors, out_weight, lat_window, lon_offset, cotangent):
    row_count, col_count, channels = queries.shape
    head_count = channels // HD
    columns = jnp.arange(col_count, dtype=jnp.int32)[None, :]
    forward_index = (columns + lon_offset[:, None]) % col_count
    backward_index = (columns - lon_offset[:, None]) % col_count
    query_view = pick_cols(queries, forward_index)
    key_view = pick_cols(key_vectors, forward_index)
    value_view = pick_cols(value_vectors, forward_index)
    grad_view = pick_cols(cotangent, forward_index)
    grad_attended = jnp.dot(grad_view.reshape(-1, channels), out_weight.T, preferred_element_type=jnp.float32)
    grad_attended = grad_attended.astype(jnp.bfloat16).reshape(row_count, col_count, channels)
    window_ids = block_ids(lat_window, col_count)
    results = lax.map(window_pass, (to_blocks(query_view, head_count), to_blocks(key_view, head_count), to_blocks(value_view, head_count), to_blocks(grad_attended, head_count), window_ids))
    attended, grad_query, grad_key, grad_value = [from_blocks(part_blocks, row_count, col_count) for part_blocks in results]
    flat = attended.reshape(-1, channels)
    mixed = jnp.dot(flat, out_weight, preferred_element_type=jnp.float32).astype(jnp.bfloat16)
    mixed = mixed.reshape(row_count, col_count, channels)
    grad_weight = jnp.dot(flat.T, grad_view.reshape(-1, channels), preferred_element_type=jnp.float32)
    return (pick_cols(mixed, backward_index), pick_cols(grad_query, backward_index), pick_cols(grad_key, backward_index), pick_cols(grad_value, backward_index), grad_weight)
```

```python
import functools

import jax
import jax.numpy as jnp
from jax import lax
from jax.experimental import pallas as pl
from jax.experimental.pallas import tpu as pltpu
from jax.sharding import PartitionSpec as P

HD = 32
WIN = 12
PAD = 16
LANES = 128
GH = LANES // HD
SUB = WIN * WIN
SLOTS = 14
BUF = 176
OWN = WIN * PAD
BF = jnp.bfloat16
F32 = jnp.float32
VMEM_LIMIT = 48 * 1024 * 1024
NN = (((1,), (0,)), ((), ()))
NT = (((1,), (1,)), ((), ()))
TN = (((0,), (0,)), ((), ()))


def dot(a, b, dims=NN):
    return lax.dot_general(a, b, dims, preferred_element_type=F32)


def passed_along(value, axis, steps):
    count = lax.axis_size(axis)
    pairs = [(source, (source + steps) % count) for source in range(count)]
    return lax.ppermute(value, axis, pairs)


def swapped(value, axis, bit):
    count = lax.axis_size(axis)
    return lax.ppermute(value, axis, [(source, source ^ bit) for source in range(count)])


def sub_layout(lat, lon, sub):
    base = 2 * WIN * (sub // 2)
    first = lat[base]
    leading = lat[base + WIN - 1] == first
    trailing = lat[base + WIN] == lat[base + 2 * WIN - 1]
    count = jnp.int32(0)
    for i in range(WIN):
        count += (lat[base + i] == first).astype(jnp.int32)
    start = jnp.where(leading, 0, jnp.where(trailing, WIN, count))
    if sub % 2 == 0:
        off = lon[base + start]
        return jnp.int32(WIN), off, off, lambda i: base + start + i
    row = lambda i: base + i + jnp.where(i >= start, WIN, 0)
    head = lat[row(0)]
    split = jnp.int32(0)
    for i in range(WIN):
        split += (lat[row(i)] == head).astype(jnp.int32)
    return split, lon[row(0)], lon[row(WIN - 1)], row


def west_groups(off):
    total = jnp.zeros_like(off)
    for g in range(4):
        total += (off <= 10 - 3 * g).astype(jnp.int32)
    return total


def column(count):
    return lax.broadcasted_iota(jnp.int32, (count, 1), 0)


def one_hot(target, width):
    lanes = lax.broadcasted_iota(jnp.int32, (target.shape[0], width), 1)
    return jnp.where(lanes == target, 1.0, 0.0).astype(BF)


def split_div(n, by):
    q = (n * ((1 << 20) // by + 1)) >> 20
    return q, n - q * by


def slot_places(split, off1, off2):
    i, u = split_div(column(BUF), SLOTS)
    off = jnp.where(i < split, off1, off2)
    real = i < WIN
    nw = west_groups(off)
    gw = jnp.zeros_like(off)
    ge = jnp.zeros_like(off)
    rest = WIN - off
    for k in range(1, 4):
        gw += (u >= k * off).astype(jnp.int32)
        ge += (u >= k * rest).astype(jnp.int32)
    west = (real & (u < nw * off), gw, u - gw * off)
    east = (real & (u < (4 - nw) * rest), nw + ge, off + u - ge * rest)
    return i, off, west, east


def pack_kernel(
    lat, lon, q_ref, k_ref, v_ref, cot_ref, w_ref,
    tab_ref, xf_ref, xg_ref, wf_ref, ef_ref, wg_ref, eg_ref, pad_ref,
):
    rows = q_ref.shape[0]
    for a, ref in enumerate((q_ref, k_ref, v_ref, cot_ref)):
        pad_ref[a, :, 0:WIN, :] = ref[...]
        pad_ref[a, :, WIN:PAD, :] = jnp.zeros((rows, PAD - WIN, ref.shape[2]), BF)
    cot = pad_ref[3].reshape(rows * PAD, -1)
    pad_ref[3] = dot(cot, w_ref[...], NT).astype(BF).reshape(rows, PAD, -1)
    for sub in range(rows // WIN):
        split, off1, off2, row = sub_layout(lat, lon, sub)
        tab_ref[sub, 0] = split
        tab_ref[sub, 1] = off1
        tab_ref[sub, 2] = off2
        for i in range(WIN):
            r = row(i)
            tab_ref[sub, 4 + i] = r
            for g in range(4):
                lanes = slice(g * LANES, (g + 1) * LANES)
                for a in range(3):
                    xf_ref[sub * 4 + g, i * PAD : (i + 1) * PAD, a * LANES : (a + 1) * LANES] = (
                        pad_ref[a, r, :, lanes]
                    )
                xg_ref[sub * 4 + g, i * PAD : (i + 1) * PAD, :] = pad_ref[3, r, :, lanes]
        i, off, west, east = slot_places(split, off1, off2)
        xf = xf_ref[sub * 4 : sub * 4 + 4].reshape(4 * OWN, 3 * LANES)
        xg = xg_ref[sub * 4 : sub * 4 + 4].reshape(4 * OWN, LANES)
        for (valid, group, col), f_ref, g_ref in ((west, wf_ref, wg_ref), (east, ef_ref, eg_ref)):
            pick = one_hot(jnp.where(valid, group * OWN + i * PAD + col, -1), 4 * OWN)
            f_ref[sub] = dot(pick, xf).astype(BF)
            g_ref[sub] = dot(pick, xg).astype(BF)


def window_pick(split, off1, off2, g):
    i, p = split_div(column(SUB), WIN)
    off = jnp.where(i < split, off1, off2)
    nw = west_groups(off)
    is_west = g < nw
    rest = WIN - off
    own = (is_west & (p < rest)) | ((~is_west) & (p >= rest))
    c = off + p - jnp.where(p >= rest, WIN, 0)
    t_own = jnp.where(own, i * PAD + c, -1)
    t_west = jnp.where(is_west & (p >= rest), i * SLOTS + g * off + (p - rest), -1)
    t_east = jnp.where((~is_west) & (p < rest), i * SLOTS + (g - nw) * rest + p, -1)
    return one_hot(t_own, OWN), one_hot(t_west, BUF), one_hot(t_east, BUF)


def own_pick(split, off1, off2, g):
    n = column(OWN)
    i, c = n >> 4, n & (PAD - 1)
    off = jnp.where(i < split, off1, off2)
    is_west = g < west_groups(off)
    local = ((is_west & (c >= off)) | ((~is_west) & (c < off))) & (c < WIN)
    p = c - off + jnp.where(c < off, WIN, 0)
    return one_hot(jnp.where(local, i * WIN + p, -1), SUB)


def far_pick(split, off1, off2, g):
    n = column(OWN)
    i, c = n >> 4, n & (PAD - 1)
    off = jnp.where(i < split, off1, off2)
    nw = west_groups(off)
    is_west = g < nw
    t_west = jnp.where(is_west & (c < off), i * SLOTS + g * off + c, -1)
    t_east = jnp.where(
        (~is_west) & (c >= off) & (c < WIN), i * SLOTS + (g - nw) * (WIN - off) + (c - off), -1
    )
    return one_hot(t_west, BUF), one_hot(t_east, BUF)


def return_pick(split, off1, off2, g):
    i, off, west, east = slot_places(split, off1, off2)
    t_west = jnp.where(west[0] & (west[1] == g), i * WIN + (WIN - off) + west[2], -1)
    t_east = jnp.where(east[0] & (east[1] == g), i * WIN + east[2] - off, -1)
    return one_hot(t_west, SUB), one_hot(t_east, SUB)


def by_head(x):
    lane = lax.broadcasted_iota(jnp.int32, (1, LANES), 1) // HD
    return jnp.concatenate(
        [x * jnp.where(lane == h, 1.0, 0.0).astype(BF) for h in range(GH)], axis=0
    )


def diagonal(full):
    return jnp.concatenate(
        [full[h * HD : (h + 1) * HD, h * SUB : (h + 1) * SUB] for h in range(GH)], axis=0
    )


def forward_kernel(
    tab, xf_ref, rw_ref, re_ref, probs_ref, win_ref, own_ref, bw_ref, be_ref, aw_ref, ae_ref
):
    sub = pl.program_id(0)
    g = pl.program_id(1)
    split, off1, off2 = tab[sub, 0], tab[sub, 1], tab[sub, 2]
    p_own, p_west, p_east = window_pick(split, off1, off2, g)
    cells = dot(p_own, xf_ref[0]) + dot(p_west, rw_ref[0]) + dot(p_east, re_ref[0])
    cells = cells.astype(BF)
    win_ref[0] = cells
    query, key, value = (cells[:, a * LANES : (a + 1) * LANES] for a in range(3))
    scores = dot(key, by_head(query), NT)
    shape = scores.shape
    edge = split * WIN
    lane = lax.broadcasted_iota(jnp.int32, (1, shape[1]), 1)
    cell = lane - split_div(lane, SUB)[0] * SUB
    in_first = jnp.where(cell < edge, 1, 0)
    key_first = jnp.where(column(SUB) < edge, 1, 0)
    scores = jnp.where(key_first == in_first, scores, -1e30)
    top = jnp.max(scores, axis=0, keepdims=True)
    rate = float(HD) ** -0.5 * 1.4426950408889634
    power = jnp.exp2((scores - top) * rate)
    probs = power * (1.0 / jnp.sum(power, axis=0, keepdims=True))
    probs = probs.astype(BF)
    probs_ref[0] = probs
    att = diagonal(dot(value, probs, TN)).astype(BF)
    own_ref[0] = dot(own_pick(split, off1, off2, g), att, NT).astype(BF)
    b_west, b_east = return_pick(split, off1, off2, g)
    back_w = dot(b_west, att, NT)
    back_e = dot(b_east, att, NT)

    @pl.when(g == 0)
    def _():
        aw_ref[...] = back_w
        ae_ref[...] = back_e

    @pl.when(g > 0)
    def _():
        aw_ref[...] += back_w
        ae_ref[...] += back_e

    @pl.when(g == 3)
    def _():
        bw_ref[0] = aw_ref[...].astype(BF)
        be_ref[0] = ae_ref[...].astype(BF)


def backward_kernel(
    tab, probs_ref, win_ref, xg_ref, rw_ref, re_ref, own_ref, bw_ref, be_ref, aw_ref, ae_ref
):
    sub = pl.program_id(0)
    g = pl.program_id(1)
    split, off1, off2 = tab[sub, 0], tab[sub, 1], tab[sub, 2]
    p_own, p_west, p_east = window_pick(split, off1, off2, g)
    grad = dot(p_own, xg_ref[0]) + dot(p_west, rw_ref[0]) + dot(p_east, re_ref[0])
    grads = by_head(grad.astype(BF))
    query, key, value = (win_ref[0, :, a * LANES : (a + 1) * LANES] for a in range(3))
    queries = by_head(query)
    probs_b = probs_ref[0]
    probs = probs_b.astype(F32)
    grad_probs = dot(value, grads, NT)
    inner = jnp.sum(probs * grad_probs, axis=0, keepdims=True)
    grad_scores = (probs * (grad_probs - inner) * float(HD) ** -0.5).astype(BF)
    grad_v = dot(probs_b, grads).astype(BF)
    grad_k = dot(grad_scores, queries).astype(BF)
    grad_q = diagonal(dot(key, grad_scores, TN)).astype(BF)

    def moved(pick):
        return jnp.concatenate(
            [dot(pick, grad_q, NT), dot(pick, grad_k), dot(pick, grad_v)], axis=1
        )

    own_ref[0] = moved(own_pick(split, off1, off2, g)).astype(BF)
    b_west, b_east = return_pick(split, off1, off2, g)
    back_w = moved(b_west)
    back_e = moved(b_east)

    @pl.when(g == 0)
    def _():
        aw_ref[...] = back_w
        ae_ref[...] = back_e

    @pl.when(g > 0)
    def _():
        aw_ref[...] += back_w
        ae_ref[...] += back_e

    @pl.when(g == 3)
    def _():
        bw_ref[0] = aw_ref[...].astype(BF)
        be_ref[0] = ae_ref[...].astype(BF)


def project_kernel(tab, own_ref, rw_ref, re_ref, w_ref, cot_ref, out_ref, dw_ref, pad_ref):
    rows = out_ref.shape[0]
    for sub in range(rows // WIN):
        split, off1, off2 = tab[sub, 0], tab[sub, 1], tab[sub, 2]
        for g in range(4):
            f_west, f_east = far_pick(split, off1, off2, g)
            full = dot(f_west, rw_ref[sub]) + dot(f_east, re_ref[sub])
            full = (full + own_ref[sub * 4 + g].astype(F32)).astype(BF).reshape(WIN, PAD, LANES)
            for i in range(WIN):
                pad_ref[0, tab[sub, 4 + i], :, g * LANES : (g + 1) * LANES] = full[i]
    att = pad_ref[0].reshape(rows * PAD, -1)
    mixed = dot(att, w_ref[...]).astype(BF).reshape(rows, PAD, -1)
    out_ref[...] = mixed[:, 0:WIN, :]
    pad_ref[1, :, 0:WIN, :] = cot_ref[...]
    pad_ref[1, :, WIN:PAD, :] = jnp.zeros((rows, PAD - WIN, cot_ref.shape[2]), BF)
    cot = pad_ref[1].reshape(rows * PAD, -1)
    dw_ref[...] = dot(att, cot, TN).astype(BF)


def place_kernel(tab, own_ref, rw_ref, re_ref, dq_ref, dk_ref, dv_ref):
    rows = dq_ref.shape[0]
    for sub in range(rows // WIN):
        split, off1, off2 = tab[sub, 0], tab[sub, 1], tab[sub, 2]
        for g in range(4):
            f_west, f_east = far_pick(split, off1, off2, g)
            full = dot(f_west, rw_ref[sub]) + dot(f_east, re_ref[sub])
            full = (full + own_ref[sub * 4 + g].astype(F32)).astype(BF)
            full = full.reshape(WIN, PAD, 3 * LANES)
            for i in range(WIN):
                for a, ref in enumerate((dq_ref, dk_ref, dv_ref)):
                    ref[tab[sub, 4 + i], :, g * LANES : (g + 1) * LANES] = full[
                        i, 0:WIN, a * LANES : (a + 1) * LANES
                    ]


def shape(*dims, kind=BF):
    return jax.ShapeDtypeStruct(dims, kind)


SMEM = pl.BlockSpec(memory_space=pltpu.SMEM)
VMEM = pl.BlockSpec(memory_space=pltpu.VMEM)
PARAMS = pltpu.CompilerParams(vmem_limit_bytes=VMEM_LIMIT)


def cost(flops, size, exps=0):
    return pl.CostEstimate(flops=int(flops), bytes_accessed=int(size), transcendentals=int(exps))


def summed(partial, axis):
    index = lax.axis_index(axis)
    bits = [1 << b for b in range(lax.axis_size(axis).bit_length() - 1)]
    for bit in bits:
        upper = (index & bit) != 0
        half = partial.shape[0] // 2
        low, high = partial[:half], partial[half:]
        far = swapped(jnp.where(upper, low, high), axis, bit)
        near = jnp.where(upper, high, low)
        partial = (near.astype(F32) + far.astype(F32)).astype(BF)
    for bit in bits[::-1]:
        upper = (index & bit) != 0
        far = swapped(partial, axis, bit)
        partial = jnp.where(
            upper, jnp.concatenate([far, partial]), jnp.concatenate([partial, far])
        )
    return partial.astype(F32)


def per_device(queries, key_vectors, value_vectors, out_weight, lat_window, lon_offset, cotangent):
    rows, cols, channels = queries.shape
    subs = rows // WIN
    steps = subs * 4
    buf_f, buf_g = shape(subs, BUF, 3 * LANES), shape(subs, BUF, LANES)
    tab, own_f, own_g, west_f, east_f, west_g, east_g = pl.pallas_call(
        pack_kernel,
        in_specs=[SMEM, SMEM] + [VMEM] * 5,
        out_specs=[SMEM] + [VMEM] * 6,
        out_shape=[
            shape(subs, 4 + WIN, kind=jnp.int32),
            shape(steps, OWN, 3 * LANES), shape(steps, OWN, LANES),
            buf_f, buf_f, buf_g, buf_g,
        ],
        scratch_shapes=[pltpu.VMEM((4, rows, PAD, channels), BF)],
        compiler_params=PARAMS,
        cost_estimate=cost(4e9, 10e6),
    )(lat_window, lon_offset, queries, key_vectors, value_vectors, cotangent, out_weight)

    from_east_f = passed_along(west_f, "lon", -1)
    from_west_f = passed_along(east_f, "lon", 1)
    from_east_g = passed_along(west_g, "lon", -1)
    from_west_g = passed_along(east_g, "lon", 1)

    step = lambda *dims: pl.BlockSpec((1,) + dims, lambda s, g: (s * 4 + g, 0, 0))
    each = lambda *dims: pl.BlockSpec((1,) + dims, lambda s, g: (s, 0, 0))
    probs, windows, own_a, back_e_a, back_w_a = pl.pallas_call(
        forward_kernel,
        grid=(subs, 4),
        in_specs=[SMEM, step(OWN, 3 * LANES), each(BUF, 3 * LANES), each(BUF, 3 * LANES)],
        out_specs=[
            step(SUB, GH * SUB), step(SUB, 3 * LANES), step(OWN, LANES),
            each(BUF, LANES), each(BUF, LANES),
        ],
        out_shape=[
            shape(steps, SUB, GH * SUB), shape(steps, SUB, 3 * LANES), shape(steps, OWN, LANES),
            buf_g, buf_g,
        ],
        scratch_shapes=[pltpu.VMEM((BUF, LANES), F32)] * 2,
        compiler_params=PARAMS,
        cost_estimate=cost(6e9, 10e6, 1.4e6),
    )(tab, own_f, from_east_f, from_west_f)

    home_w_a = passed_along(back_e_a, "lon", 1)
    home_e_a = passed_along(back_w_a, "lon", -1)

    own_d, back_e_d, back_w_d = pl.pallas_call(
        backward_kernel,
        grid=(subs, 4),
        in_specs=[
            SMEM, step(SUB, GH * SUB), step(SUB, 3 * LANES), step(OWN, LANES),
            each(BUF, LANES), each(BUF, LANES),
        ],
        out_specs=[step(OWN, 3 * LANES), each(BUF, 3 * LANES), each(BUF, 3 * LANES)],
        out_shape=[shape(steps, OWN, 3 * LANES), buf_f, buf_f],
        scratch_shapes=[pltpu.VMEM((BUF, 3 * LANES), F32)] * 2,
        compiler_params=PARAMS,
        cost_estimate=cost(8e9, 10e6),
    )(tab, probs, windows, own_g, from_east_g, from_west_g)

    home_w_d = passed_along(back_e_d, "lon", 1)
    home_e_d = passed_along(back_w_d, "lon", -1)

    whole = shape(rows, cols, channels)
    mixed, partial = pl.pallas_call(
        project_kernel,
        in_specs=[SMEM] + [VMEM] * 5,
        out_specs=[VMEM] * 2,
        out_shape=[whole, shape(channels, channels)],
        scratch_shapes=[pltpu.VMEM((2, rows, PAD, channels), BF)],
        compiler_params=PARAMS,
        cost_estimate=cost(2e9, 4e6),
    )(tab, own_a, home_w_a, home_e_a, out_weight, cotangent)

    grads = pl.pallas_call(
        place_kernel,
        in_specs=[SMEM] + [VMEM] * 3,
        out_specs=[VMEM] * 3,
        out_shape=[whole] * 3,
        compiler_params=PARAMS,
        cost_estimate=cost(2e9, 6e6),
    )(tab, own_d, home_w_d, home_e_d)

    return (mixed, grads[0], grads[1], grads[2], summed(partial, "lon"))


def solution(mesh):
    placed = (
        P("groups", "lon", None),
        P("groups", "lon", None),
        P("groups", "lon", None),
        P(),
        P("groups"),
        P("groups"),
        P("groups", "lon", None),
    )
    return jax.shard_map(
        per_device,
        mesh=mesh,
        in_specs=placed,
        out_specs=(
            P("groups", "lon", None),
            P("groups", "lon", None),
            P("groups", "lon", None),
            P("groups", "lon", None),
            P("groups", None),
        ),
        check_vma=False,
    )
```

```python
import functools

import jax
import jax.numpy as jnp
from jax import lax
from jax.experimental import pallas as pl
from jax.experimental.pallas import tpu as pltpu
from jax.sharding import PartitionSpec as P

HD = 32
WIN = 12
PAD = 16
LANES = 128
GH = LANES // HD
SUB = WIN * WIN
SLOTS = 14
BUF = 176
OWN = WIN * PAD
BF = jnp.bfloat16
F32 = jnp.float32
MIB = 1024 * 1024
NN = (((1,), (0,)), ((), ()))
NT = (((1,), (1,)), ((), ()))
TN = (((0,), (0,)), ((), ()))


def dot(a, b, dims=NN):
    return lax.dot_general(a, b, dims, preferred_element_type=F32)


def passed_along(value, axis, steps):
    count = lax.axis_size(axis)
    pairs = [(source, (source + steps) % count) for source in range(count)]
    return lax.ppermute(value, axis, pairs)


def swapped(value, axis, bit):
    count = lax.axis_size(axis)
    return lax.ppermute(value, axis, [(source, source ^ bit) for source in range(count)])


def sub_layout(lat, lon, sub):
    base = 2 * WIN * (sub // 2)
    first = lat[base]
    leading = lat[base + WIN - 1] == first
    trailing = lat[base + WIN] == lat[base + 2 * WIN - 1]
    count = jnp.int32(0)
    for i in range(WIN):
        count += (lat[base + i] == first).astype(jnp.int32)
    start = jnp.where(leading, 0, jnp.where(trailing, WIN, count))
    if sub % 2 == 0:
        off = lon[base + start]
        return jnp.int32(WIN), off, off, lambda i: base + start + i
    row = lambda i: base + i + jnp.where(i >= start, WIN, 0)
    head = lat[row(0)]
    split = jnp.int32(0)
    for i in range(WIN):
        split += (lat[row(i)] == head).astype(jnp.int32)
    return split, lon[row(0)], lon[row(WIN - 1)], row


def west_groups(off):
    total = jnp.zeros_like(off)
    for g in range(4):
        total += (off <= 10 - 3 * g).astype(jnp.int32)
    return total


def column(count):
    return lax.broadcasted_iota(jnp.int32, (count, 1), 0)


def one_hot(target, width):
    lanes = lax.broadcasted_iota(jnp.int32, (target.shape[0], width), 1)
    return jnp.where(lanes == target, 1.0, 0.0).astype(BF)


def split_div(n, by):
    q = (n * ((1 << 20) // by + 1)) >> 20
    return q, n - q * by


def slot_places(split, off1, off2):
    i, u = split_div(column(BUF), SLOTS)
    off = jnp.where(i < split, off1, off2)
    real = i < WIN
    nw = west_groups(off)
    gw = jnp.zeros_like(off)
    ge = jnp.zeros_like(off)
    rest = WIN - off
    for k in range(1, 4):
        gw += (u >= k * off).astype(jnp.int32)
        ge += (u >= k * rest).astype(jnp.int32)
    west = (real & (u < nw * off), gw, u - gw * off)
    east = (real & (u < (4 - nw) * rest), nw + ge, off + u - ge * rest)
    return i, off, west, east


def own_rows(x, pad_ref, at):
    x = jnp.swapaxes(x, 0, 1)
    pad_ref[at, :, 0:WIN, :] = x
    pad_ref[at, :, WIN:PAD, :] = jnp.zeros((x.shape[0], PAD - WIN, x.shape[2]), BF)


def send_pick(split, off1, off2):
    i, off, west, east = slot_places(split, off1, off2)
    targets = [
        jnp.where(valid, group * OWN + i * PAD + col, -1) for valid, group, col in (west, east)
    ]
    return one_hot(jnp.concatenate(targets, axis=0), 4 * OWN)


def pack_kernel(lat, lon, q_ref, k_ref, v_ref, tab_ref, own_ref, west_ref, east_ref, pad_ref):
    rows = q_ref.shape[1]
    for a, ref in enumerate((q_ref, k_ref, v_ref)):
        own_rows(ref[...], pad_ref, a)
    for sub in range(rows // WIN):
        split, off1, off2, row = sub_layout(lat, lon, sub)
        tab_ref[sub, 0] = split
        tab_ref[sub, 1] = off1
        tab_ref[sub, 2] = off2
        for i in range(WIN):
            r = row(i)
            tab_ref[sub, 4 + i] = r
            for g in range(4):
                for a in range(3):
                    own_ref[sub * 4 + g, i * PAD : (i + 1) * PAD, a * LANES : (a + 1) * LANES] = (
                        pad_ref[a, r, :, g * LANES : (g + 1) * LANES]
                    )
        own = own_ref[sub * 4 : sub * 4 + 4].reshape(4 * OWN, 3 * LANES)
        sent = dot(send_pick(split, off1, off2), own).astype(BF)
        west_ref[sub] = sent[0:BUF]
        east_ref[sub] = sent[BUF:]


def pack_grad_kernel(tab, cot_ref, w_ref, own_ref, west_ref, east_ref, pad_ref):
    cols, rows, channels = cot_ref.shape
    grad = dot(cot_ref[...].reshape(cols * rows, channels), w_ref[...], NT).astype(BF)
    own_rows(grad.reshape(cols, rows, channels), pad_ref, 0)
    for sub in range(rows // WIN):
        for i in range(WIN):
            r = tab[sub, 4 + i]
            for g in range(4):
                own_ref[sub * 4 + g, i * PAD : (i + 1) * PAD, :] = (
                    pad_ref[0, r, :, g * LANES : (g + 1) * LANES]
                )
        own = own_ref[sub * 4 : sub * 4 + 4].reshape(4 * OWN, LANES)
        sent = dot(send_pick(tab[sub, 0], tab[sub, 1], tab[sub, 2]), own).astype(BF)
        west_ref[sub] = sent[0:BUF]
        east_ref[sub] = sent[BUF:]


def prepare_kernel(tab, own_ref, win_ref, pick_ref, fw_ref, fe_ref, move_ref, hw_ref, he_ref):
    sub = pl.program_id(0)
    split, off1, off2 = tab[sub, 0], tab[sub, 1], tab[sub, 2]
    i, p = split_div(column(SUB), WIN)
    off = jnp.where(i < split, off1, off2)
    nw = west_groups(off)
    rest = WIN - off
    c = off + p - jnp.where(p >= rest, WIN, 0)
    n = column(OWN)
    j, k = n >> 4, n & (PAD - 1)
    off_o = jnp.where(j < split, off1, off2)
    nw_o = west_groups(off_o)
    before = k < off_o
    real = k < WIN
    p_o = k - off_o + jnp.where(before, WIN, 0)
    _, off_s, west, east = slot_places(split, off1, off2)
    i_s = split_div(column(BUF), SLOTS)[0]
    for g in range(4):
        is_west = g < nw
        own = (is_west & (p < rest)) | ((~is_west) & (p >= rest))
        pick = one_hot(jnp.where(own, i * PAD + c, -1), OWN)
        win_ref[g] = dot(pick, own_ref[g]).astype(BF)
        pick_ref[g] = pick
        t_west = jnp.where(is_west & (p >= rest), i * SLOTS + g * off + (p - rest), -1)
        t_east = jnp.where((~is_west) & (p < rest), i * SLOTS + (g - nw) * rest + p, -1)
        fw_ref[g] = one_hot(t_west, BUF)
        fe_ref[g] = one_hot(t_east, BUF)
        t_west = jnp.where(west[0] & (west[1] == g), i_s * WIN + (WIN - off_s) + west[2], -1)
        t_east = jnp.where(east[0] & (east[1] == g), i_s * WIN + east[2] - off_s, -1)
        is_west = g < nw_o
        local = ((is_west & (~before)) | ((~is_west) & before)) & real
        move_ref[g, 0:BUF] = one_hot(t_west, SUB)
        move_ref[g, BUF : 2 * BUF] = one_hot(t_east, SUB)
        move_ref[g, 2 * BUF :] = one_hot(jnp.where(local, j * WIN + p_o, -1), SUB)
        t_west = jnp.where(is_west & before, j * SLOTS + g * off_o + k, -1)
        t_east = jnp.where(
            (~is_west) & (~before) & real, j * SLOTS + (g - nw_o) * (WIN - off_o) + (k - off_o), -1
        )
        hw_ref[g] = one_hot(t_west, BUF)
        he_ref[g] = one_hot(t_east, BUF)


def by_head(x):
    lane = lax.broadcasted_iota(jnp.int32, (1, LANES), 1) // HD
    return jnp.concatenate(
        [x * jnp.where(lane == h, 1.0, 0.0).astype(BF) for h in range(GH)], axis=0
    )


def diagonal(full):
    return jnp.concatenate(
        [full[h * HD : (h + 1) * HD, h * SUB : (h + 1) * SUB] for h in range(GH)], axis=0
    )


def forward_kernel(
    tab, win_ref, fw_ref, fe_ref, move_ref, rw_ref, re_ref,
    probs_ref, cells_ref, own_ref, bw_ref, be_ref,
):
    sub = pl.program_id(0)
    edge = tab[sub, 0] * WIN
    lane = lax.broadcasted_iota(jnp.int32, (1, GH * SUB), 1)
    cell = lane - split_div(lane, SUB)[0] * SUB
    in_first = jnp.where(cell < edge, 1, 0)
    key_first = jnp.where(column(SUB) < edge, 1, 0)
    rate = float(HD) ** -0.5 * 1.4426950408889634
    far = dot(fw_ref[...].reshape(4 * SUB, BUF), rw_ref[0])
    far += dot(fe_ref[...].reshape(4 * SUB, BUF), re_ref[0])
    for g in range(4):
        cells_ref[g] = (win_ref[g].astype(F32) + far[g * SUB : (g + 1) * SUB]).astype(BF)
    scores = [
        dot(cells_ref[g, :, LANES : 2 * LANES], by_head(cells_ref[g, :, 0:LANES]), NT)
        for g in range(4)
    ]
    for g in range(4):
        x = jnp.where(key_first == in_first, scores[g], -1e30)
        power = jnp.exp2((x - jnp.max(x, axis=0, keepdims=True)) * rate)
        probs_ref[g] = (power * (1.0 / jnp.sum(power, axis=0, keepdims=True))).astype(BF)
    full = [dot(cells_ref[g, :, 2 * LANES :], probs_ref[g], TN) for g in range(4)]
    att = [diagonal(x).astype(BF) for x in full]
    moved = [dot(move_ref[g], att[g], NT) for g in range(4)]
    for g in range(4):
        own_ref[g] = moved[g][2 * BUF :].astype(BF)
    back = (moved[0] + moved[1]) + (moved[2] + moved[3])
    bw_ref[0] = back[0:BUF].astype(BF)
    be_ref[0] = back[BUF : 2 * BUF].astype(BF)


def backward_kernel(
    probs_ref, cells_ref, og_ref, pick_ref, fw_ref, fe_ref, move_ref, rw_ref, re_ref,
    own_ref, bw_ref, be_ref,
):
    grads = []
    far = dot(fw_ref[...].reshape(4 * SUB, BUF), rw_ref[0])
    far += dot(fe_ref[...].reshape(4 * SUB, BUF), re_ref[0])
    for g in range(4):
        grads.append(by_head((dot(pick_ref[g], og_ref[g]) + far[g * SUB : (g + 1) * SUB]).astype(BF)))
    grad_probs = [dot(cells_ref[g, :, 2 * LANES :], grads[g], NT) for g in range(4)]
    grad_v = [dot(probs_ref[g], grads[g]).astype(BF) for g in range(4)]
    grad_scores = []
    for g in range(4):
        probs = probs_ref[g].astype(F32)
        inner = jnp.sum(probs * grad_probs[g], axis=0, keepdims=True)
        grad_scores.append((probs * (grad_probs[g] - inner) * float(HD) ** -0.5).astype(BF))
    grad_k = [dot(grad_scores[g], by_head(cells_ref[g, :, 0:LANES])).astype(BF) for g in range(4)]
    full = [dot(cells_ref[g, :, LANES : 2 * LANES], grad_scores[g], TN) for g in range(4)]
    grad_q = [diagonal(x).astype(BF) for x in full]
    back = None
    for g in range(4):
        pick = move_ref[g]
        pair = jnp.concatenate([grad_k[g], grad_v[g]], axis=1)
        moved = jnp.concatenate([dot(pick, grad_q[g], NT), dot(pick, pair)], axis=1)
        own_ref[g] = moved[2 * BUF :].astype(BF)
        far = moved[0 : 2 * BUF]
        back = far if back is None else back + far
    bw_ref[0] = back[0:BUF].astype(BF)
    be_ref[0] = back[BUF:].astype(BF)


def project_kernel(
    tab, own_ref, hw_ref, he_ref, rw_ref, re_ref, w_ref, cot_ref, out_ref, dw_ref, pad_ref
):
    cols, rows, channels = out_ref.shape
    for sub in range(rows // WIN):
        for g in range(4):
            s = sub * 4 + g
            full = dot(hw_ref[s], rw_ref[sub]) + dot(he_ref[s], re_ref[sub])
            full = (full + own_ref[s].astype(F32)).astype(BF).reshape(WIN, PAD, LANES)
            for i in range(WIN):
                pad_ref[tab[sub, 4 + i], :, g * LANES : (g + 1) * LANES] = full[i]
    att = jnp.swapaxes(pad_ref[:, 0:WIN, :], 0, 1).reshape(cols * rows, channels)
    out_ref[...] = dot(att, w_ref[...]).astype(BF).reshape(cols, rows, channels)
    dw_ref[...] = dot(att, cot_ref[...].reshape(cols * rows, channels), TN).astype(BF)


def place_kernel(tab, own_ref, hw_ref, he_ref, rw_ref, re_ref, dq_ref, dk_ref, dv_ref, pad_ref):
    cols, rows, channels = dq_ref.shape
    for sub in range(rows // WIN):
        for g in range(4):
            s = sub * 4 + g
            full = dot(hw_ref[s], rw_ref[sub]) + dot(he_ref[s], re_ref[sub])
            full = (full + own_ref[s].astype(F32)).astype(BF).reshape(WIN, PAD, 3 * LANES)
            for i in range(WIN):
                for a in range(3):
                    pad_ref[a, tab[sub, 4 + i], :, g * LANES : (g + 1) * LANES] = full[
                        i, :, a * LANES : (a + 1) * LANES
                    ]
    for a, ref in enumerate((dq_ref, dk_ref, dv_ref)):
        ref[...] = jnp.swapaxes(pad_ref[a, :, 0:WIN, :], 0, 1)


def shape(*dims, kind=BF):
    return jax.ShapeDtypeStruct(dims, kind)


SMEM = pl.BlockSpec(memory_space=pltpu.SMEM)
VMEM = pl.BlockSpec(memory_space=pltpu.VMEM)


def params(mib):
    return pltpu.CompilerParams(vmem_limit_bytes=mib * MIB)


WHOLE, SHARED = params(63), params(20)


def cost(flops, size, exps=0):
    return pl.CostEstimate(flops=int(flops), bytes_accessed=int(size), transcendentals=int(exps))


def sum_stages(count):
    stages, bit = [(1, 2)], 2
    while bit < count:
        ways = 4 if 4 * bit <= count else 2
        stages.append((bit, ways))
        bit *= ways
    return stages


def scattered_sum(partial, axis, bit, ways):
    place = (lax.axis_index(axis) // bit) % ways
    part = partial.shape[0] // ways
    piece = lambda k: lax.dynamic_slice_in_dim(partial, (place ^ k) * part, part, 0)
    total = piece(0).astype(F32)
    for far in [swapped(piece(k), axis, k * bit) for k in range(ways - 1, 0, -1)]:
        total = total + far.astype(F32)
    return total.astype(BF)


def gathered_back(partial, axis, bit, ways):
    place = (lax.axis_index(axis) // bit) % ways
    parts = [partial] + [swapped(partial, axis, k * bit) for k in range(1, ways)]
    rows = []
    for slot in range(ways):
        x = parts[0]
        for k in range(1, ways):
            x = jnp.where(place == slot ^ k, parts[k], x)
        rows.append(x)
    return jnp.concatenate(rows)


def turned(x):
    return jnp.transpose(x, (1, 0, 2))


def per_device(queries, key_vectors, value_vectors, out_weight, lat_window, lon_offset, cotangent):
    rows, cols, channels = queries.shape
    subs = rows // WIN
    steps = subs * 4
    buf_f, buf_g = shape(subs, BUF, 3 * LANES), shape(subs, BUF, LANES)
    cot_t = turned(cotangent)
    tab, own, west_f, east_f = pl.pallas_call(
        pack_kernel,
        in_specs=[SMEM, SMEM] + [VMEM] * 3,
        out_specs=[SMEM] + [VMEM] * 3,
        out_shape=[
            shape(subs, 4 + WIN, kind=jnp.int32), shape(steps, OWN, 3 * LANES), buf_f, buf_f,
        ],
        scratch_shapes=[pltpu.VMEM((3, rows, PAD, channels), BF)],
        compiler_params=WHOLE,
        cost_estimate=cost(4e9, 8e6),
    )(lat_window, lon_offset, turned(queries), turned(key_vectors), turned(value_vectors))

    from_east_f = passed_along(west_f, "lon", -1)
    from_west_f = passed_along(east_f, "lon", 1)

    own_g, west_g, east_g = pl.pallas_call(
        pack_grad_kernel,
        in_specs=[SMEM] + [VMEM] * 2,
        out_specs=[VMEM] * 3,
        out_shape=[shape(steps, OWN, LANES), buf_g, buf_g],
        scratch_shapes=[pltpu.VMEM((1, rows, PAD, channels), BF)],
        compiler_params=WHOLE,
        cost_estimate=cost(4e9, 3e6),
    )(tab, cot_t, out_weight)

    from_east_g = passed_along(west_g, "lon", -1)
    from_west_g = passed_along(east_g, "lon", 1)

    group = lambda *dims: pl.BlockSpec((4,) + dims, lambda s: (s, 0, 0))
    each = lambda *dims: pl.BlockSpec((1,) + dims, lambda s: (s, 0, 0))
    windows, pick, far_w, far_e, move, home_w, home_e = pl.pallas_call(
        prepare_kernel,
        grid=(subs,),
        in_specs=[SMEM, group(OWN, 3 * LANES)],
        out_specs=[
            group(SUB, 3 * LANES), group(SUB, OWN), group(SUB, BUF), group(SUB, BUF), group(2 * BUF + OWN, SUB),
            group(OWN, BUF), group(OWN, BUF),
        ],
        out_shape=[
            shape(steps, SUB, 3 * LANES), shape(steps, SUB, OWN), shape(steps, SUB, BUF),
            shape(steps, SUB, BUF),
            shape(steps, 2 * BUF + OWN, SUB), shape(steps, OWN, BUF), shape(steps, OWN, BUF),
        ],
        compiler_params=SHARED,
        cost_estimate=cost(6e9, 20e6),
    )(tab, own)

    probs, cells, own_a, back_e_a, back_w_a = pl.pallas_call(
        forward_kernel,
        grid=(subs,),
        in_specs=[
            SMEM, group(SUB, 3 * LANES), group(SUB, BUF), group(SUB, BUF),
            group(2 * BUF + OWN, SUB), each(BUF, 3 * LANES), each(BUF, 3 * LANES),
        ],
        out_specs=[
            group(SUB, GH * SUB), group(SUB, 3 * LANES), group(OWN, LANES),
            each(BUF, LANES), each(BUF, LANES),
        ],
        out_shape=[
            shape(steps, SUB, GH * SUB), shape(steps, SUB, 3 * LANES), shape(steps, OWN, LANES),
            buf_g, buf_g,
        ],
        compiler_params=SHARED,
        cost_estimate=cost(6e9, 10e6, 1.4e6),
    )(tab, windows, far_w, far_e, move, from_east_f, from_west_f)

    home_w_a = passed_along(back_e_a, "lon", 1)
    home_e_a = passed_along(back_w_a, "lon", -1)

    own_d, back_e_d, back_w_d = pl.pallas_call(
        backward_kernel,
        grid=(subs,),
        in_specs=[
            group(SUB, GH * SUB), group(SUB, 3 * LANES),
            group(OWN, LANES), group(SUB, OWN), group(SUB, BUF), group(SUB, BUF),
            group(2 * BUF + OWN, SUB), each(BUF, LANES), each(BUF, LANES),
        ],
        out_specs=[group(OWN, 3 * LANES), each(BUF, 3 * LANES), each(BUF, 3 * LANES)],
        out_shape=[shape(steps, OWN, 3 * LANES), buf_f, buf_f],
        compiler_params=SHARED,
        cost_estimate=cost(8e9, 10e6),
    )(probs, cells, own_g, pick, far_w, far_e, move, from_east_g, from_west_g)

    home_w_d = passed_along(back_e_d, "lon", 1)
    home_e_d = passed_along(back_w_d, "lon", -1)

    home_w_a, home_e_a, own_d = lax.optimization_barrier((home_w_a, home_e_a, own_d))
    whole = shape(cols, rows, channels)
    mixed, partial = pl.pallas_call(
        project_kernel,
        in_specs=[SMEM] + [VMEM] * 7,
        out_specs=[VMEM] * 2,
        out_shape=[whole, shape(channels, channels)],
        scratch_shapes=[pltpu.VMEM((rows, PAD, channels), BF)],
        compiler_params=SHARED,
        cost_estimate=cost(2e9, 4e6),
    )(tab, own_a, home_w, home_e, home_w_a, home_e_a, out_weight, cot_t)

    stages = sum_stages(lax.axis_size("lon"))
    for bit, ways in stages:
        partial = scattered_sum(partial, "lon", bit, ways)
    partial, home_w_d, home_e_d = lax.optimization_barrier((partial, home_w_d, home_e_d))
    partial = gathered_back(partial, "lon", *stages[-1])
    grads = pl.pallas_call(
        place_kernel,
        in_specs=[SMEM] + [VMEM] * 5,
        out_specs=[VMEM] * 3,
        out_shape=[whole] * 3,
        scratch_shapes=[pltpu.VMEM((3, rows, PAD, channels), BF)],
        compiler_params=SHARED,
        cost_estimate=cost(2e9, 6e6),
    )(tab, own_d, home_w, home_e, home_w_d, home_e_d)

    partial, grads = lax.optimization_barrier((partial, grads))
    for bit, ways in stages[-2::-1]:
        partial = gathered_back(partial, "lon", bit, ways)
    total = partial.astype(F32)

    return (turned(mixed),) + tuple(turned(x) for x in grads) + (total,)


def solution(mesh):
    placed = (
        P("groups", "lon", None),
        P("groups", "lon", None),
        P("groups", "lon", None),
        P(),
        P("groups"),
        P("groups"),
        P("groups", "lon", None),
    )
    return jax.shard_map(
        per_device,
        mesh=mesh,
        in_specs=placed,
        out_specs=(
            P("groups", "lon", None),
            P("groups", "lon", None),
            P("groups", "lon", None),
            P("groups", "lon", None),
            P("groups", None),
        ),
        check_vma=False,
    )
```

```python
import functools

import jax
import jax.numpy as jnp
from jax import lax
from jax.experimental import pallas as pl
from jax.experimental.pallas import tpu as pltpu
from jax.sharding import PartitionSpec as P

HD = 32
WIN = 12
PAD = 16
LANES = 128
GH = LANES // HD
SUB = WIN * WIN
SLOTS = 14
BUF = 176
OWN = WIN * PAD
BF = jnp.bfloat16
F32 = jnp.float32
MIB = 1024 * 1024
NN = (((1,), (0,)), ((), ()))
NT = (((1,), (1,)), ((), ()))
TN = (((0,), (0,)), ((), ()))


def dot(a, b, dims=NN):
    return lax.dot_general(a, b, dims, preferred_element_type=F32)


def passed_along(value, axis, steps):
    count = lax.axis_size(axis)
    pairs = [(source, (source + steps) % count) for source in range(count)]
    return lax.ppermute(value, axis, pairs)


def swapped(value, axis, bit):
    count = lax.axis_size(axis)
    return lax.ppermute(value, axis, [(source, source ^ bit) for source in range(count)])


def sub_layout(lat, lon, sub):
    base = 2 * WIN * (sub // 2)
    first = lat[base]
    leading = lat[base + WIN - 1] == first
    trailing = lat[base + WIN] == lat[base + 2 * WIN - 1]
    count = jnp.int32(0)
    for i in range(WIN):
        count += (lat[base + i] == first).astype(jnp.int32)
    start = jnp.where(leading, 0, jnp.where(trailing, WIN, count))
    if sub % 2 == 0:
        off = lon[base + start]
        return jnp.int32(WIN), off, off, lambda i: base + start + i
    row = lambda i: base + i + jnp.where(i >= start, WIN, 0)
    head = lat[row(0)]
    split = jnp.int32(0)
    for i in range(WIN):
        split += (lat[row(i)] == head).astype(jnp.int32)
    return split, lon[row(0)], lon[row(WIN - 1)], row


def west_groups(off):
    total = jnp.zeros_like(off)
    for g in range(4):
        total += (off <= 10 - 3 * g).astype(jnp.int32)
    return total


def column(count):
    return lax.broadcasted_iota(jnp.int32, (count, 1), 0)


def one_hot(target, width):
    lanes = lax.broadcasted_iota(jnp.int32, (target.shape[0], width), 1)
    return jnp.where(lanes == target, 1.0, 0.0).astype(BF)


def split_div(n, by):
    q = (n * ((1 << 20) // by + 1)) >> 20
    return q, n - q * by


def slot_places(split, off1, off2):
    i, u = split_div(column(BUF), SLOTS)
    off = jnp.where(i < split, off1, off2)
    real = i < WIN
    nw = west_groups(off)
    gw = jnp.zeros_like(off)
    ge = jnp.zeros_like(off)
    rest = WIN - off
    for k in range(1, 4):
        gw += (u >= k * off).astype(jnp.int32)
        ge += (u >= k * rest).astype(jnp.int32)
    west = (real & (u < nw * off), gw, u - gw * off)
    east = (real & (u < (4 - nw) * rest), nw + ge, off + u - ge * rest)
    return i, off, west, east


def own_rows(x, pad_ref, at):
    x = jnp.swapaxes(x, 0, 1)
    pad_ref[at, :, 0:WIN, :] = x
    pad_ref[at, :, WIN:PAD, :] = jnp.zeros((x.shape[0], PAD - WIN, x.shape[2]), BF)


def send_pick(split, off1, off2):
    i, off, west, east = slot_places(split, off1, off2)
    targets = [
        jnp.where(valid, group * OWN + i * PAD + col, -1) for valid, group, col in (west, east)
    ]
    return one_hot(jnp.concatenate(targets, axis=0), 4 * OWN)


def pack_kernel(lat, lon, q_ref, k_ref, v_ref, tab_ref, own_ref, west_ref, east_ref, pad_ref):
    rows = q_ref.shape[1]
    for a, ref in enumerate((q_ref, k_ref, v_ref)):
        own_rows(ref[...], pad_ref, a)
    for sub in range(rows // WIN):
        split, off1, off2, row = sub_layout(lat, lon, sub)
        tab_ref[sub, 0] = split
        tab_ref[sub, 1] = off1
        tab_ref[sub, 2] = off2
        for i in range(WIN):
            r = row(i)
            tab_ref[sub, 4 + i] = r
            for g in range(4):
                for a in range(3):
                    own_ref[sub * 4 + g, i * PAD : (i + 1) * PAD, a * LANES : (a + 1) * LANES] = (
                        pad_ref[a, r, :, g * LANES : (g + 1) * LANES]
                    )
        own = own_ref[sub * 4 : sub * 4 + 4].reshape(4 * OWN, 3 * LANES)
        sent = dot(send_pick(split, off1, off2), own).astype(BF)
        west_ref[sub] = sent[0:BUF]
        east_ref[sub] = sent[BUF:]


def pack_grad_kernel(tab, cot_ref, w_ref, own_ref, west_ref, east_ref, pad_ref):
    cols, rows, channels = cot_ref.shape
    grad = dot(cot_ref[...].reshape(cols * rows, channels), w_ref[...], NT).astype(BF)
    own_rows(grad.reshape(cols, rows, channels), pad_ref, 0)
    for sub in range(rows // WIN):
        for i in range(WIN):
            r = tab[sub, 4 + i]
            for g in range(4):
                own_ref[sub * 4 + g, i * PAD : (i + 1) * PAD, :] = (
                    pad_ref[0, r, :, g * LANES : (g + 1) * LANES]
                )
        own = own_ref[sub * 4 : sub * 4 + 4].reshape(4 * OWN, LANES)
        sent = dot(send_pick(tab[sub, 0], tab[sub, 1], tab[sub, 2]), own).astype(BF)
        west_ref[sub] = sent[0:BUF]
        east_ref[sub] = sent[BUF:]


def prepare_kernel(tab, own_ref, win_ref, pick_ref, fw_ref, fe_ref, move_ref, hw_ref, he_ref):
    sub = pl.program_id(0)
    split, off1, off2 = tab[sub, 0], tab[sub, 1], tab[sub, 2]
    i, p = split_div(column(SUB), WIN)
    off = jnp.where(i < split, off1, off2)
    nw = west_groups(off)
    rest = WIN - off
    c = off + p - jnp.where(p >= rest, WIN, 0)
    n = column(OWN)
    j, k = n >> 4, n & (PAD - 1)
    off_o = jnp.where(j < split, off1, off2)
    nw_o = west_groups(off_o)
    before = k < off_o
    real = k < WIN
    p_o = k - off_o + jnp.where(before, WIN, 0)
    _, off_s, west, east = slot_places(split, off1, off2)
    i_s = split_div(column(BUF), SLOTS)[0]
    for g in range(4):
        is_west = g < nw
        own = (is_west & (p < rest)) | ((~is_west) & (p >= rest))
        pick = one_hot(jnp.where(own, i * PAD + c, -1), OWN)
        win_ref[g] = dot(pick, own_ref[g]).astype(BF)
        pick_ref[g] = pick
        t_west = jnp.where(is_west & (p >= rest), i * SLOTS + g * off + (p - rest), -1)
        t_east = jnp.where((~is_west) & (p < rest), i * SLOTS + (g - nw) * rest + p, -1)
        fw_ref[g] = one_hot(t_west, BUF)
        fe_ref[g] = one_hot(t_east, BUF)
        t_west = jnp.where(west[0] & (west[1] == g), i_s * WIN + (WIN - off_s) + west[2], -1)
        t_east = jnp.where(east[0] & (east[1] == g), i_s * WIN + east[2] - off_s, -1)
        is_west = g < nw_o
        local = ((is_west & (~before)) | ((~is_west) & before)) & real
        move_ref[g, 0:BUF] = one_hot(t_west, SUB)
        move_ref[g, BUF : 2 * BUF] = one_hot(t_east, SUB)
        move_ref[g, 2 * BUF :] = one_hot(jnp.where(local, j * WIN + p_o, -1), SUB)
        t_west = jnp.where(is_west & before, j * SLOTS + g * off_o + k, -1)
        t_east = jnp.where(
            (~is_west) & (~before) & real, j * SLOTS + (g - nw_o) * (WIN - off_o) + (k - off_o), -1
        )
        hw_ref[g] = one_hot(t_west, BUF)
        he_ref[g] = one_hot(t_east, BUF)


def by_head(x):
    lane = lax.broadcasted_iota(jnp.int32, (1, LANES), 1) // HD
    return jnp.concatenate(
        [x * jnp.where(lane == h, 1.0, 0.0).astype(BF) for h in range(GH)], axis=0
    )


def diagonal(full):
    return jnp.concatenate(
        [full[h * HD : (h + 1) * HD, h * SUB : (h + 1) * SUB] for h in range(GH)], axis=0
    )


def forward_kernel(
    tab, win_ref, fw_ref, fe_ref, move_ref, rw_ref, re_ref,
    probs_ref, cells_ref, own_ref, bw_ref, be_ref,
):
    sub = pl.program_id(0)
    edge = tab[sub, 0] * WIN
    lane = lax.broadcasted_iota(jnp.int32, (1, GH * SUB), 1)
    cell = lane - split_div(lane, SUB)[0] * SUB
    in_first = jnp.where(cell < edge, 1, 0)
    key_first = jnp.where(column(SUB) < edge, 1, 0)
    rate = float(HD) ** -0.5 * 1.4426950408889634
    far = dot(fw_ref[...].reshape(4 * SUB, BUF), rw_ref[0])
    far += dot(fe_ref[...].reshape(4 * SUB, BUF), re_ref[0])
    for g in range(4):
        cells_ref[g] = (win_ref[g].astype(F32) + far[g * SUB : (g + 1) * SUB]).astype(BF)
    scores = [
        dot(cells_ref[g, :, LANES : 2 * LANES], by_head(cells_ref[g, :, 0:LANES]), NT)
        for g in range(4)
    ]
    for g in range(4):
        x = jnp.where(key_first == in_first, scores[g], -1e30)
        power = jnp.exp2((x - jnp.max(x, axis=0, keepdims=True)) * rate)
        probs_ref[g] = (power * (1.0 / jnp.sum(power, axis=0, keepdims=True))).astype(BF)
    full = [dot(cells_ref[g, :, 2 * LANES :], probs_ref[g], TN) for g in range(4)]
    att = [diagonal(x).astype(BF) for x in full]
    moved = [dot(move_ref[g], att[g], NT) for g in range(4)]
    for g in range(4):
        own_ref[g] = moved[g][2 * BUF :].astype(BF)
    back = (moved[0] + moved[1]) + (moved[2] + moved[3])
    bw_ref[0] = back[0:BUF].astype(BF)
    be_ref[0] = back[BUF : 2 * BUF].astype(BF)


def backward_kernel(
    probs_ref, cells_ref, og_ref, pick_ref, fw_ref, fe_ref, move_ref, rw_ref, re_ref,
    own_ref, bw_ref, be_ref,
):
    grads = []
    far = dot(fw_ref[...].reshape(4 * SUB, BUF), rw_ref[0])
    far += dot(fe_ref[...].reshape(4 * SUB, BUF), re_ref[0])
    for g in range(4):
        grads.append(by_head((dot(pick_ref[g], og_ref[g]) + far[g * SUB : (g + 1) * SUB]).astype(BF)))
    grad_probs = [dot(cells_ref[g, :, 2 * LANES :], grads[g], NT) for g in range(4)]
    grad_v = [dot(probs_ref[g], grads[g]).astype(BF) for g in range(4)]
    grad_scores = []
    for g in range(4):
        probs = probs_ref[g].astype(F32)
        inner = jnp.sum(probs * grad_probs[g], axis=0, keepdims=True)
        inner = inner / jnp.sum(probs, axis=0, keepdims=True)
        grad_scores.append((probs * (grad_probs[g] - inner) * float(HD) ** -0.5).astype(BF))
    grad_k = [dot(grad_scores[g], by_head(cells_ref[g, :, 0:LANES])).astype(BF) for g in range(4)]
    full = [dot(cells_ref[g, :, LANES : 2 * LANES], grad_scores[g], TN) for g in range(4)]
    grad_q = [diagonal(x).astype(BF) for x in full]
    back = None
    for g in range(4):
        pick = move_ref[g]
        pair = jnp.concatenate([grad_k[g], grad_v[g]], axis=1)
        moved = jnp.concatenate([dot(pick, grad_q[g], NT), dot(pick, pair)], axis=1)
        own_ref[g] = moved[2 * BUF :].astype(BF)
        far = moved[0 : 2 * BUF]
        back = far if back is None else back + far
    bw_ref[0] = back[0:BUF].astype(BF)
    be_ref[0] = back[BUF:].astype(BF)


def project_kernel(
    tab, own_ref, hw_ref, he_ref, rw_ref, re_ref, w_ref, cot_ref, out_ref, dw_ref, pad_ref
):
    cols, rows, channels = out_ref.shape
    for sub in range(rows // WIN):
        for g in range(4):
            s = sub * 4 + g
            full = dot(hw_ref[s], rw_ref[sub]) + dot(he_ref[s], re_ref[sub])
            full = (full + own_ref[s].astype(F32)).astype(BF).reshape(WIN, PAD, LANES)
            for i in range(WIN):
                pad_ref[tab[sub, 4 + i], :, g * LANES : (g + 1) * LANES] = full[i]
    att = jnp.swapaxes(pad_ref[:, 0:WIN, :], 0, 1).reshape(cols * rows, channels)
    out_ref[...] = dot(att, w_ref[...]).astype(BF).reshape(cols, rows, channels)
    dw_ref[...] = dot(att, cot_ref[...].reshape(cols * rows, channels), TN).astype(BF)


def place_kernel(tab, own_ref, hw_ref, he_ref, rw_ref, re_ref, dq_ref, dk_ref, dv_ref, pad_ref):
    sub = pl.program_id(0)
    for g in range(4):
        full = dot(hw_ref[g], rw_ref[0]) + dot(he_ref[g], re_ref[0])
        full = (full + own_ref[g].astype(F32)).astype(BF).reshape(WIN, PAD, 3 * LANES)
        for i in range(WIN):
            row = tab[sub, 4 + i]
            for a in range(3):
                pad_ref[a, row, :, g * LANES : (g + 1) * LANES] = full[
                    i, :, a * LANES : (a + 1) * LANES
                ]

    @pl.when(sub == pl.num_programs(0) - 1)
    def _():
        for a, ref in enumerate((dq_ref, dk_ref, dv_ref)):
            ref[...] = jnp.swapaxes(pad_ref[a, :, 0:WIN, :], 0, 1)


def shape(*dims, kind=BF):
    return jax.ShapeDtypeStruct(dims, kind)


SMEM = pl.BlockSpec(memory_space=pltpu.SMEM)
VMEM = pl.BlockSpec(memory_space=pltpu.VMEM)


def params(mib):
    return pltpu.CompilerParams(vmem_limit_bytes=mib * MIB)


WHOLE, SHARED = params(63), params(20)


def cost(flops, size, exps=0):
    return pl.CostEstimate(flops=int(flops), bytes_accessed=int(size), transcendentals=int(exps))


def sum_stages(count):
    stages, bit = [(1, 2)], 2
    while bit < count:
        ways = 4 if 4 * bit <= count else 2
        stages.append((bit, ways))
        bit *= ways
    return stages


def scattered_sum(partial, axis, bit, ways):
    place = (lax.axis_index(axis) // bit) % ways
    part = partial.shape[0] // ways
    piece = lambda k: lax.dynamic_slice_in_dim(partial, (place ^ k) * part, part, 0)
    total = piece(0).astype(F32)
    for far in [swapped(piece(k), axis, k * bit) for k in range(ways - 1, 0, -1)]:
        total = total + far.astype(F32)
    return total.astype(BF)


def gathered_back(partial, axis, bit, ways):
    place = (lax.axis_index(axis) // bit) % ways
    parts = [partial] + [swapped(partial, axis, k * bit) for k in range(1, ways)]
    rows = []
    for slot in range(ways):
        x = parts[0]
        for k in range(1, ways):
            x = jnp.where(place == slot ^ k, parts[k], x)
        rows.append(x)
    return jnp.concatenate(rows)


def turned(x):
    return jnp.transpose(x, (1, 0, 2))


def per_device(queries, key_vectors, value_vectors, out_weight, lat_window, lon_offset, cotangent):
    rows, cols, channels = queries.shape
    subs = rows // WIN
    steps = subs * 4
    buf_f, buf_g = shape(subs, BUF, 3 * LANES), shape(subs, BUF, LANES)
    cot_t = turned(cotangent)
    tab, own, west_f, east_f = pl.pallas_call(
        pack_kernel,
        in_specs=[SMEM, SMEM] + [VMEM] * 3,
        out_specs=[SMEM] + [VMEM] * 3,
        out_shape=[
            shape(subs, 4 + WIN, kind=jnp.int32), shape(steps, OWN, 3 * LANES), buf_f, buf_f,
        ],
        scratch_shapes=[pltpu.VMEM((3, rows, PAD, channels), BF)],
        compiler_params=WHOLE,
        cost_estimate=cost(4e9, 8e6),
    )(lat_window, lon_offset, turned(queries), turned(key_vectors), turned(value_vectors))

    from_east_f = passed_along(west_f, "lon", -1)
    from_west_f = passed_along(east_f, "lon", 1)

    own_g, west_g, east_g = pl.pallas_call(
        pack_grad_kernel,
        in_specs=[SMEM] + [VMEM] * 2,
        out_specs=[VMEM] * 3,
        out_shape=[shape(steps, OWN, LANES), buf_g, buf_g],
        scratch_shapes=[pltpu.VMEM((1, rows, PAD, channels), BF)],
        compiler_params=WHOLE,
        cost_estimate=cost(4e9, 3e6),
    )(tab, cot_t, out_weight)

    from_east_g = passed_along(west_g, "lon", -1)
    from_west_g = passed_along(east_g, "lon", 1)

    group = lambda *dims: pl.BlockSpec((4,) + dims, lambda s: (s, 0, 0))
    each = lambda *dims: pl.BlockSpec((1,) + dims, lambda s: (s, 0, 0))
    windows, pick, far_w, far_e, move, home_w, home_e = pl.pallas_call(
        prepare_kernel,
        grid=(subs,),
        in_specs=[SMEM, group(OWN, 3 * LANES)],
        out_specs=[
            group(SUB, 3 * LANES), group(SUB, OWN), group(SUB, BUF), group(SUB, BUF), group(2 * BUF + OWN, SUB),
            group(OWN, BUF), group(OWN, BUF),
        ],
        out_shape=[
            shape(steps, SUB, 3 * LANES), shape(steps, SUB, OWN), shape(steps, SUB, BUF),
            shape(steps, SUB, BUF),
            shape(steps, 2 * BUF + OWN, SUB), shape(steps, OWN, BUF), shape(steps, OWN, BUF),
        ],
        compiler_params=SHARED,
        cost_estimate=cost(6e9, 20e6),
    )(tab, own)

    probs, cells, own_a, back_e_a, back_w_a = pl.pallas_call(
        forward_kernel,
        grid=(subs,),
        in_specs=[
            SMEM, group(SUB, 3 * LANES), group(SUB, BUF), group(SUB, BUF),
            group(2 * BUF + OWN, SUB), each(BUF, 3 * LANES), each(BUF, 3 * LANES),
        ],
        out_specs=[
            group(SUB, GH * SUB), group(SUB, 3 * LANES), group(OWN, LANES),
            each(BUF, LANES), each(BUF, LANES),
        ],
        out_shape=[
            shape(steps, SUB, GH * SUB), shape(steps, SUB, 3 * LANES), shape(steps, OWN, LANES),
            buf_g, buf_g,
        ],
        compiler_params=SHARED,
        cost_estimate=cost(6e9, 10e6, 1.4e6),
    )(tab, windows, far_w, far_e, move, from_east_f, from_west_f)

    home_w_a = passed_along(back_e_a, "lon", 1)
    home_e_a = passed_along(back_w_a, "lon", -1)

    own_d, back_e_d, back_w_d = pl.pallas_call(
        backward_kernel,
        grid=(subs,),
        in_specs=[
            group(SUB, GH * SUB), group(SUB, 3 * LANES),
            group(OWN, LANES), group(SUB, OWN), group(SUB, BUF), group(SUB, BUF),
            group(2 * BUF + OWN, SUB), each(BUF, LANES), each(BUF, LANES),
        ],
        out_specs=[group(OWN, 3 * LANES), each(BUF, 3 * LANES), each(BUF, 3 * LANES)],
        out_shape=[shape(steps, OWN, 3 * LANES), buf_f, buf_f],
        compiler_params=SHARED,
        cost_estimate=cost(8e9, 10e6),
    )(probs, cells, own_g, pick, far_w, far_e, move, from_east_g, from_west_g)

    home_w_d = passed_along(back_e_d, "lon", 1)
    home_e_d = passed_along(back_w_d, "lon", -1)

    home_w_a, home_e_a, own_d = lax.optimization_barrier((home_w_a, home_e_a, own_d))
    whole = shape(cols, rows, channels)
    mixed, partial = pl.pallas_call(
        project_kernel,
        in_specs=[SMEM] + [VMEM] * 7,
        out_specs=[VMEM] * 2,
        out_shape=[whole, shape(channels, channels)],
        scratch_shapes=[pltpu.VMEM((rows, PAD, channels), BF)],
        compiler_params=SHARED,
        cost_estimate=cost(2e9, 4e6),
    )(tab, own_a, home_w, home_e, home_w_a, home_e_a, out_weight, cot_t)

    stages = sum_stages(lax.axis_size("lon"))
    for bit, ways in stages:
        partial = scattered_sum(partial, "lon", bit, ways)
    partial, home_w_d, home_e_d = lax.optimization_barrier((partial, home_w_d, home_e_d))
    partial = gathered_back(partial, "lon", *stages[-1])
    partial, home_w_d, home_e_d = lax.optimization_barrier((partial, home_w_d, home_e_d))
    grads = pl.pallas_call(
        place_kernel,
        grid=(subs,),
        in_specs=[
            SMEM, group(OWN, 3 * LANES), group(OWN, BUF), group(OWN, BUF),
            each(BUF, 3 * LANES), each(BUF, 3 * LANES),
        ],
        out_specs=[VMEM] * 3,
        out_shape=[whole] * 3,
        scratch_shapes=[pltpu.VMEM((3, rows, PAD, channels), BF)],
        compiler_params=WHOLE,
        cost_estimate=cost(4e9, 6e6),
    )(tab, own_d, home_w, home_e, home_w_d, home_e_d)

    for bit, ways in stages[-2:0:-1]:
        partial = gathered_back(partial, "lon", bit, ways)
    partial, grads = lax.optimization_barrier((partial, grads))
    total = gathered_back(partial, "lon", *stages[0]).astype(F32)

    return (turned(mixed),) + tuple(turned(x) for x in grads) + (total,)


def solution(mesh):
    placed = (
        P("groups", "lon", None),
        P("groups", "lon", None),
        P("groups", "lon", None),
        P(),
        P("groups"),
        P("groups"),
        P("groups", "lon", None),
    )
    return jax.shard_map(
        per_device,
        mesh=mesh,
        in_specs=placed,
        out_specs=(
            P("groups", "lon", None),
            P("groups", "lon", None),
            P("groups", "lon", None),
            P("groups", "lon", None),
            P("groups", None),
        ),
        check_vma=False,
    )
```

```python
import functools

import jax
import jax.numpy as jnp
from jax import lax
from jax.experimental import pallas as pl
from jax.experimental.pallas import tpu as pltpu
from jax.sharding import PartitionSpec as P

HD = 32
WIN = 12
PAD = 16
LANES = 128
GH = LANES // HD
SUB = WIN * WIN
SLOTS = 14
BUF = 176
OWN = WIN * PAD
BF = jnp.bfloat16
F32 = jnp.float32
MIB = 1024 * 1024
NN = (((1,), (0,)), ((), ()))
NT = (((1,), (1,)), ((), ()))
TN = (((0,), (0,)), ((), ()))


def dot(a, b, dims=NN):
    return lax.dot_general(a, b, dims, preferred_element_type=F32)


def passed_along(value, axis, steps):
    count = lax.axis_size(axis)
    pairs = [(source, (source + steps) % count) for source in range(count)]
    return lax.ppermute(value, axis, pairs)


def swapped(value, axis, bit):
    count = lax.axis_size(axis)
    return lax.ppermute(value, axis, [(source, source ^ bit) for source in range(count)])


def sub_layout(lat, lon, sub):
    base = 2 * WIN * (sub // 2)
    first = lat[base]
    leading = lat[base + WIN - 1] == first
    trailing = lat[base + WIN] == lat[base + 2 * WIN - 1]
    count = jnp.int32(0)
    for i in range(WIN):
        count += (lat[base + i] == first).astype(jnp.int32)
    start = jnp.where(leading, 0, jnp.where(trailing, WIN, count))
    if sub % 2 == 0:
        off = lon[base + start]
        return jnp.int32(WIN), off, off, lambda i: base + start + i
    row = lambda i: base + i + jnp.where(i >= start, WIN, 0)
    head = lat[row(0)]
    split = jnp.int32(0)
    for i in range(WIN):
        split += (lat[row(i)] == head).astype(jnp.int32)
    return split, lon[row(0)], lon[row(WIN - 1)], row


def west_groups(off):
    total = jnp.zeros_like(off)
    for g in range(4):
        total += (off <= 10 - 3 * g).astype(jnp.int32)
    return total


def column(count):
    return lax.broadcasted_iota(jnp.int32, (count, 1), 0)


def one_hot(target, width):
    lanes = lax.broadcasted_iota(jnp.int32, (target.shape[0], width), 1)
    return jnp.where(lanes == target, 1.0, 0.0).astype(BF)


def split_div(n, by):
    q = (n * ((1 << 20) // by + 1)) >> 20
    return q, n - q * by


def slot_places(split, off1, off2):
    i, u = split_div(column(BUF), SLOTS)
    off = jnp.where(i < split, off1, off2)
    real = i < WIN
    nw = west_groups(off)
    gw = jnp.zeros_like(off)
    ge = jnp.zeros_like(off)
    rest = WIN - off
    for k in range(1, 4):
        gw += (u >= k * off).astype(jnp.int32)
        ge += (u >= k * rest).astype(jnp.int32)
    west = (real & (u < nw * off), gw, u - gw * off)
    east = (real & (u < (4 - nw) * rest), nw + ge, off + u - ge * rest)
    return i, off, west, east


def own_rows(x, pad_ref, at):
    x = jnp.swapaxes(x, 0, 1)
    pad_ref[at, :, 0:WIN, :] = x
    pad_ref[at, :, WIN:PAD, :] = jnp.zeros((x.shape[0], PAD - WIN, x.shape[2]), BF)


def send_pick(split, off1, off2):
    i, off, west, east = slot_places(split, off1, off2)
    targets = [
        jnp.where(valid, group * OWN + i * PAD + col, -1) for valid, group, col in (west, east)
    ]
    return one_hot(jnp.concatenate(targets, axis=0), 4 * OWN)


def pack_kernel(lat, lon, q_ref, k_ref, v_ref, tab_ref, own_ref, west_ref, east_ref, pad_ref):
    rows = q_ref.shape[1]
    for a, ref in enumerate((q_ref, k_ref, v_ref)):
        own_rows(ref[...], pad_ref, a)
    for sub in range(rows // WIN):
        split, off1, off2, row = sub_layout(lat, lon, sub)
        tab_ref[sub, 0] = split
        tab_ref[sub, 1] = off1
        tab_ref[sub, 2] = off2
        for i in range(WIN):
            r = row(i)
            tab_ref[sub, 4 + i] = r
            for g in range(4):
                for a in range(3):
                    own_ref[sub * 4 + g, i * PAD : (i + 1) * PAD, a * LANES : (a + 1) * LANES] = (
                        pad_ref[a, r, :, g * LANES : (g + 1) * LANES]
                    )
        own = own_ref[sub * 4 : sub * 4 + 4].reshape(4 * OWN, 3 * LANES)
        sent = dot(send_pick(split, off1, off2), own).astype(BF)
        west_ref[sub] = sent[0:BUF]
        east_ref[sub] = sent[BUF:]


def pack_grad_kernel(tab, cot_ref, w_ref, own_ref, west_ref, east_ref, pad_ref):
    cols, rows, channels = cot_ref.shape
    grad = dot(cot_ref[...].reshape(cols * rows, channels), w_ref[...], NT).astype(BF)
    own_rows(grad.reshape(cols, rows, channels), pad_ref, 0)
    for sub in range(rows // WIN):
        for i in range(WIN):
            r = tab[sub, 4 + i]
            for g in range(4):
                own_ref[sub * 4 + g, i * PAD : (i + 1) * PAD, :] = (
                    pad_ref[0, r, :, g * LANES : (g + 1) * LANES]
                )
        own = own_ref[sub * 4 : sub * 4 + 4].reshape(4 * OWN, LANES)
        sent = dot(send_pick(tab[sub, 0], tab[sub, 1], tab[sub, 2]), own).astype(BF)
        west_ref[sub] = sent[0:BUF]
        east_ref[sub] = sent[BUF:]


def prepare_kernel(tab, own_ref, win_ref, pick_ref, fw_ref, fe_ref, move_ref, hw_ref, he_ref):
    sub = pl.program_id(0)
    split, off1, off2 = tab[sub, 0], tab[sub, 1], tab[sub, 2]
    i, p = split_div(column(SUB), WIN)
    off = jnp.where(i < split, off1, off2)
    nw = west_groups(off)
    rest = WIN - off
    c = off + p - jnp.where(p >= rest, WIN, 0)
    n = column(OWN)
    j, k = n >> 4, n & (PAD - 1)
    off_o = jnp.where(j < split, off1, off2)
    nw_o = west_groups(off_o)
    before = k < off_o
    real = k < WIN
    p_o = k - off_o + jnp.where(before, WIN, 0)
    _, off_s, west, east = slot_places(split, off1, off2)
    i_s = split_div(column(BUF), SLOTS)[0]
    for g in range(4):
        is_west = g < nw
        own = (is_west & (p < rest)) | ((~is_west) & (p >= rest))
        pick = one_hot(jnp.where(own, i * PAD + c, -1), OWN)
        win_ref[g] = dot(pick, own_ref[g]).astype(BF)
        pick_ref[g] = pick
        t_west = jnp.where(is_west & (p >= rest), i * SLOTS + g * off + (p - rest), -1)
        t_east = jnp.where((~is_west) & (p < rest), i * SLOTS + (g - nw) * rest + p, -1)
        fw_ref[g] = one_hot(t_west, BUF)
        fe_ref[g] = one_hot(t_east, BUF)
        t_west = jnp.where(west[0] & (west[1] == g), i_s * WIN + (WIN - off_s) + west[2], -1)
        t_east = jnp.where(east[0] & (east[1] == g), i_s * WIN + east[2] - off_s, -1)
        is_west = g < nw_o
        local = ((is_west & (~before)) | ((~is_west) & before)) & real
        move_ref[g, 0:BUF] = one_hot(t_west, SUB)
        move_ref[g, BUF : 2 * BUF] = one_hot(t_east, SUB)
        move_ref[g, 2 * BUF :] = one_hot(jnp.where(local, j * WIN + p_o, -1), SUB)
        t_west = jnp.where(is_west & before, j * SLOTS + g * off_o + k, -1)
        t_east = jnp.where(
            (~is_west) & (~before) & real, j * SLOTS + (g - nw_o) * (WIN - off_o) + (k - off_o), -1
        )
        hw_ref[g] = one_hot(t_west, BUF)
        he_ref[g] = one_hot(t_east, BUF)


def by_head(x):
    lane = lax.broadcasted_iota(jnp.int32, (1, LANES), 1) // HD
    return jnp.concatenate(
        [x * jnp.where(lane == h, 1.0, 0.0).astype(BF) for h in range(GH)], axis=0
    )


def diagonal(full):
    return jnp.concatenate(
        [full[h * HD : (h + 1) * HD, h * SUB : (h + 1) * SUB] for h in range(GH)], axis=0
    )


def forward_kernel(
    tab, win_ref, fw_ref, fe_ref, move_ref, rw_ref, re_ref,
    probs_ref, cells_ref, own_ref, bw_ref, be_ref,
):
    sub = pl.program_id(0)
    edge = tab[sub, 0] * WIN
    lane = lax.broadcasted_iota(jnp.int32, (1, GH * SUB), 1)
    cell = lane - split_div(lane, SUB)[0] * SUB
    in_first = jnp.where(cell < edge, 1, 0)
    key_first = jnp.where(column(SUB) < edge, 1, 0)
    rate = float(HD) ** -0.5 * 1.4426950408889634
    far = dot(fw_ref[...].reshape(4 * SUB, BUF), rw_ref[0])
    far += dot(fe_ref[...].reshape(4 * SUB, BUF), re_ref[0])
    for g in range(4):
        cells_ref[g] = (win_ref[g].astype(F32) + far[g * SUB : (g + 1) * SUB]).astype(BF)
    scores = [
        dot(cells_ref[g, :, LANES : 2 * LANES], by_head(cells_ref[g, :, 0:LANES]), NT)
        for g in range(4)
    ]
    for g in range(4):
        x = jnp.where(key_first == in_first, scores[g], -1e30)
        power = jnp.exp2((x - jnp.max(x, axis=0, keepdims=True)) * rate)
        probs_ref[g] = (power * (1.0 / jnp.sum(power, axis=0, keepdims=True))).astype(BF)
    full = [dot(cells_ref[g, :, 2 * LANES :], probs_ref[g], TN) for g in range(4)]
    att = [diagonal(x).astype(BF) for x in full]
    moved = [dot(move_ref[g], att[g], NT) for g in range(4)]
    for g in range(4):
        own_ref[g] = moved[g][2 * BUF :].astype(BF)
    back = (moved[0] + moved[1]) + (moved[2] + moved[3])
    bw_ref[0] = back[0:BUF].astype(BF)
    be_ref[0] = back[BUF : 2 * BUF].astype(BF)


def backward_kernel(
    probs_ref, cells_ref, og_ref, pick_ref, fw_ref, fe_ref, move_ref, rw_ref, re_ref,
    own_ref, bw_ref, be_ref,
):
    grads = []
    far = dot(fw_ref[...].reshape(4 * SUB, BUF), rw_ref[0])
    far += dot(fe_ref[...].reshape(4 * SUB, BUF), re_ref[0])
    for g in range(4):
        grads.append(by_head((dot(pick_ref[g], og_ref[g]) + far[g * SUB : (g + 1) * SUB]).astype(BF)))
    grad_probs = [dot(cells_ref[g, :, 2 * LANES :], grads[g], NT) for g in range(4)]
    grad_v = [dot(probs_ref[g], grads[g]).astype(BF) for g in range(4)]
    grad_scores = []
    for g in range(4):
        probs = probs_ref[g].astype(F32)
        inner = jnp.sum(probs * grad_probs[g], axis=0, keepdims=True)
        inner = inner / jnp.sum(probs, axis=0, keepdims=True)
        grad_scores.append((probs * (grad_probs[g] - inner) * float(HD) ** -0.5).astype(BF))
    grad_k = [dot(grad_scores[g], by_head(cells_ref[g, :, 0:LANES])).astype(BF) for g in range(4)]
    full = [dot(cells_ref[g, :, LANES : 2 * LANES], grad_scores[g], TN) for g in range(4)]
    grad_q = [diagonal(x).astype(BF) for x in full]
    back = None
    for g in range(4):
        pick = move_ref[g]
        pair = jnp.concatenate([grad_k[g], grad_v[g]], axis=1)
        moved = jnp.concatenate([dot(pick, grad_q[g], NT), dot(pick, pair)], axis=1)
        own_ref[g] = moved[2 * BUF :].astype(BF)
        far = moved[0 : 2 * BUF]
        back = far if back is None else back + far
    bw_ref[0] = back[0:BUF].astype(BF)
    be_ref[0] = back[BUF:].astype(BF)


def project_kernel(
    tab, own_ref, hw_ref, he_ref, rw_ref, re_ref, w_ref, cot_ref, out_ref, dw_ref, pad_ref
):
    cols, rows, channels = out_ref.shape
    for sub in range(rows // WIN):
        for g in range(4):
            s = sub * 4 + g
            full = dot(hw_ref[s], rw_ref[sub]) + dot(he_ref[s], re_ref[sub])
            full = (full + own_ref[s].astype(F32)).astype(BF).reshape(WIN, PAD, LANES)
            for i in range(WIN):
                pad_ref[tab[sub, 4 + i], :, g * LANES : (g + 1) * LANES] = full[i]
    att = jnp.swapaxes(pad_ref[:, 0:WIN, :], 0, 1).reshape(cols * rows, channels)
    out_ref[...] = dot(att, w_ref[...]).astype(BF).reshape(cols, rows, channels)
    dw_ref[...] = dot(att, cot_ref[...].reshape(cols * rows, channels), TN).astype(BF)


def place_kernel(tab, own_ref, hw_ref, he_ref, rw_ref, re_ref, dq_ref, dk_ref, dv_ref, pad_ref):
    sub = pl.program_id(0)
    for g in range(4):
        full = dot(hw_ref[g], rw_ref[0]) + dot(he_ref[g], re_ref[0])
        full = (full + own_ref[g].astype(F32)).astype(BF).reshape(WIN, PAD, 3 * LANES)
        for i in range(WIN):
            row = tab[sub, 4 + i]
            for a in range(3):
                pad_ref[a, row, :, g * LANES : (g + 1) * LANES] = full[
                    i, :, a * LANES : (a + 1) * LANES
                ]

    @pl.when(sub == pl.num_programs(0) - 1)
    def _():
        for a, ref in enumerate((dq_ref, dk_ref, dv_ref)):
            ref[...] = jnp.swapaxes(pad_ref[a, :, 0:WIN, :], 0, 1)


def shape(*dims, kind=BF):
    return jax.ShapeDtypeStruct(dims, kind)


SMEM = pl.BlockSpec(memory_space=pltpu.SMEM)
VMEM = pl.BlockSpec(memory_space=pltpu.VMEM)


def params(mib):
    return pltpu.CompilerParams(vmem_limit_bytes=mib * MIB)


WHOLE, SHARED = params(63), params(20)


def cost(flops, size, exps=0):
    return pl.CostEstimate(flops=int(flops), bytes_accessed=int(size), transcendentals=int(exps))


def sum_stages(count):
    stages, bit = [(1, 2)], 2
    while bit < count:
        ways = 4 if bit > 2 and 4 * bit <= count else 2
        stages.append((bit, ways))
        bit *= ways
    return stages


def scattered_sum(partial, axis, bit, ways):
    place = (lax.axis_index(axis) // bit) % ways
    part = partial.shape[0] // ways
    piece = lambda k: lax.dynamic_slice_in_dim(partial, (place ^ k) * part, part, 0)
    total = piece(0).astype(F32)
    for far in [swapped(piece(k), axis, k * bit) for k in range(ways - 1, 0, -1)]:
        total = total + far.astype(F32)
    return total.astype(BF)


def gathered_back(partial, axis, bit, ways):
    place = (lax.axis_index(axis) // bit) % ways
    parts = [partial] + [swapped(partial, axis, k * bit) for k in range(1, ways)]
    rows = []
    for slot in range(ways):
        x = parts[0]
        for k in range(1, ways):
            x = jnp.where(place == slot ^ k, parts[k], x)
        rows.append(x)
    return jnp.concatenate(rows)


def turned(x):
    return jnp.transpose(x, (1, 0, 2))


def per_device(queries, key_vectors, value_vectors, out_weight, lat_window, lon_offset, cotangent):
    rows, cols, channels = queries.shape
    subs = rows // WIN
    steps = subs * 4
    buf_f, buf_g = shape(subs, BUF, 3 * LANES), shape(subs, BUF, LANES)
    cot_t = turned(cotangent)
    tab, own, west_f, east_f = pl.pallas_call(
        pack_kernel,
        in_specs=[SMEM, SMEM] + [VMEM] * 3,
        out_specs=[SMEM] + [VMEM] * 3,
        out_shape=[
            shape(subs, 4 + WIN, kind=jnp.int32), shape(steps, OWN, 3 * LANES), buf_f, buf_f,
        ],
        scratch_shapes=[pltpu.VMEM((3, rows, PAD, channels), BF)],
        compiler_params=WHOLE,
        cost_estimate=cost(4e9, 8e6),
    )(lat_window, lon_offset, turned(queries), turned(key_vectors), turned(value_vectors))

    from_east_f = passed_along(west_f, "lon", -1)
    from_west_f = passed_along(east_f, "lon", 1)

    own_g, west_g, east_g = pl.pallas_call(
        pack_grad_kernel,
        in_specs=[SMEM] + [VMEM] * 2,
        out_specs=[VMEM] * 3,
        out_shape=[shape(steps, OWN, LANES), buf_g, buf_g],
        scratch_shapes=[pltpu.VMEM((1, rows, PAD, channels), BF)],
        compiler_params=WHOLE,
        cost_estimate=cost(4e9, 3e6),
    )(tab, cot_t, out_weight)

    from_east_g = passed_along(west_g, "lon", -1)
    from_west_g = passed_along(east_g, "lon", 1)

    group = lambda *dims: pl.BlockSpec((4,) + dims, lambda s: (s, 0, 0))
    each = lambda *dims: pl.BlockSpec((1,) + dims, lambda s: (s, 0, 0))
    windows, pick, far_w, far_e, move, home_w, home_e = pl.pallas_call(
        prepare_kernel,
        grid=(subs,),
        in_specs=[SMEM, group(OWN, 3 * LANES)],
        out_specs=[
            group(SUB, 3 * LANES), group(SUB, OWN), group(SUB, BUF), group(SUB, BUF), group(2 * BUF + OWN, SUB),
            group(OWN, BUF), group(OWN, BUF),
        ],
        out_shape=[
            shape(steps, SUB, 3 * LANES), shape(steps, SUB, OWN), shape(steps, SUB, BUF),
            shape(steps, SUB, BUF),
            shape(steps, 2 * BUF + OWN, SUB), shape(steps, OWN, BUF), shape(steps, OWN, BUF),
        ],
        compiler_params=SHARED,
        cost_estimate=cost(6e9, 20e6),
    )(tab, own)

    probs, cells, own_a, back_e_a, back_w_a = pl.pallas_call(
        forward_kernel,
        grid=(subs,),
        in_specs=[
            SMEM, group(SUB, 3 * LANES), group(SUB, BUF), group(SUB, BUF),
            group(2 * BUF + OWN, SUB), each(BUF, 3 * LANES), each(BUF, 3 * LANES),
        ],
        out_specs=[
            group(SUB, GH * SUB), group(SUB, 3 * LANES), group(OWN, LANES),
            each(BUF, LANES), each(BUF, LANES),
        ],
        out_shape=[
            shape(steps, SUB, GH * SUB), shape(steps, SUB, 3 * LANES), shape(steps, OWN, LANES),
            buf_g, buf_g,
        ],
        compiler_params=SHARED,
        cost_estimate=cost(6e9, 10e6, 1.4e6),
    )(tab, windows, far_w, far_e, move, from_east_f, from_west_f)

    home_w_a = passed_along(back_e_a, "lon", 1)
    home_e_a = passed_along(back_w_a, "lon", -1)

    own_d, back_e_d, back_w_d = pl.pallas_call(
        backward_kernel,
        grid=(subs,),
        in_specs=[
            group(SUB, GH * SUB), group(SUB, 3 * LANES),
            group(OWN, LANES), group(SUB, OWN), group(SUB, BUF), group(SUB, BUF),
            group(2 * BUF + OWN, SUB), each(BUF, LANES), each(BUF, LANES),
        ],
        out_specs=[group(OWN, 3 * LANES), each(BUF, 3 * LANES), each(BUF, 3 * LANES)],
        out_shape=[shape(steps, OWN, 3 * LANES), buf_f, buf_f],
        compiler_params=SHARED,
        cost_estimate=cost(8e9, 10e6),
    )(probs, cells, own_g, pick, far_w, far_e, move, from_east_g, from_west_g)

    home_w_d = passed_along(back_e_d, "lon", 1)
    home_e_d = passed_along(back_w_d, "lon", -1)

    home_w_a, home_e_a, own_d = lax.optimization_barrier((home_w_a, home_e_a, own_d))
    whole = shape(cols, rows, channels)
    mixed, partial = pl.pallas_call(
        project_kernel,
        in_specs=[SMEM] + [VMEM] * 7,
        out_specs=[VMEM] * 2,
        out_shape=[whole, shape(channels, channels)],
        scratch_shapes=[pltpu.VMEM((rows, PAD, channels), BF)],
        compiler_params=SHARED,
        cost_estimate=cost(2e9, 4e6),
    )(tab, own_a, home_w, home_e, home_w_a, home_e_a, out_weight, cot_t)

    stages = sum_stages(lax.axis_size("lon"))
    for bit, ways in stages:
        partial = scattered_sum(partial, "lon", bit, ways)
    partial, home_w_d, home_e_d = lax.optimization_barrier((partial, home_w_d, home_e_d))
    partial = gathered_back(partial, "lon", *stages[-1])
    partial, home_w_d, home_e_d = lax.optimization_barrier((partial, home_w_d, home_e_d))
    grads = pl.pallas_call(
        place_kernel,
        grid=(subs,),
        in_specs=[
            SMEM, group(OWN, 3 * LANES), group(OWN, BUF), group(OWN, BUF),
            each(BUF, 3 * LANES), each(BUF, 3 * LANES),
        ],
        out_specs=[VMEM] * 3,
        out_shape=[whole] * 3,
        scratch_shapes=[pltpu.VMEM((3, rows, PAD, channels), BF)],
        compiler_params=WHOLE,
        cost_estimate=cost(4e9, 6e6),
    )(tab, own_d, home_w, home_e, home_w_d, home_e_d)

    for bit, ways in stages[-2:0:-1]:
        partial = gathered_back(partial, "lon", bit, ways)
    partial, grads = lax.optimization_barrier((partial, grads))
    total = gathered_back(partial, "lon", *stages[0]).astype(F32)

    return (turned(mixed),) + tuple(turned(x) for x in grads) + (total,)


def solution(mesh):
    placed = (
        P("groups", "lon", None),
        P("groups", "lon", None),
        P("groups", "lon", None),
        P(),
        P("groups"),
        P("groups"),
        P("groups", "lon", None),
    )
    return jax.shard_map(
        per_device,
        mesh=mesh,
        in_specs=placed,
        out_specs=(
            P("groups", "lon", None),
            P("groups", "lon", None),
            P("groups", "lon", None),
            P("groups", "lon", None),
            P("groups", None),
        ),
        check_vma=False,
    )
```
